256 devices in a mesh: section: 4 (over z_hi), seq: 64 (over z_lo, x, y, core).
Axes of the slice: x: 4, y: 4, z: 8 (z_hi: 4, z_lo: 2; z = z_hi * 2 + z_lo), core: 2. Of those that a mesh axis runs over, the one named last changes fastest.
Arguments:
- video_saved: bfloat16 [4, 2, 4096, 1536], P('section', None, 'seq'), may hold values from -30 to 30
- audio_saved: bfloat16 [4, 2, 2048, 1536], P('section', None, 'seq'), may hold values from -6 to 6
- video_cotangent: bfloat16 [2, 4096, 1536], P(None, 'seq'), may hold values from -6 to 6
- audio_cotangent: bfloat16 [2, 2048, 1536], P(None, 'seq'), may hold values from -6 to 6
- modulation: float32 [4, 4, 1536], P('section'), may hold values from 0.25 to 1.75
- video_window: int32 [64, 2], P('seq'), may hold values from 0 to 256, as said below
- audio_window: int32 [64, 2], P('seq'), may hold values from 0 to 256, as said below
Outputs:
- video_grad: bfloat16 [4, 2, 4096, 1536], P('section', None, 'seq')
- audio_grad: bfloat16 [4, 2, 2048, 1536], P('section', None, 'seq')
- modulation_grad: float32 [4, 4, 1536], P('section')
The draws below stay inside these ranges and needn't reach their ends.
Inputs may be any that keep to these rules, and one draw needn't show every extreme that they name: `video_window`: row i: the window of shard i in audio blocks; it holds blocks 4i - 1 to 4i + 4 clipped to the sequence and lies within 4i - 2 to 4i + 6 clipped to the sequence; some shard's window spans that whole range. `audio_window`: row i: the window of shard i in video blocks, with the same bounds.
All inputs are finite; a program needn't handle non-finite values.
Results may differ from the reference program's by a relative error of at most 0.012.
Values may be sent and summed in bfloat16 or wider, within the bound.
No kernel may reach another device: no remote copies, remote signals or barrier semaphores. Data moves between devices by JAX's collectives and lax.ppermute only.
A program may use at most 128 MiB of HBM per device.

```python
import jax
import jax.numpy as jnp
from jax import lax

HDIM = 128
D = 1536
VID_DEV = 64
AUD_DEV = 32
MB = 2
VID_TOKENS = 4096
AUD_TOKENS = 2048
N_SECTION = 4
N_SEQ = 64


def shared_audio(key):
    return jax.random.normal(key, (N_SECTION, MB, AUD_TOKENS, D), jnp.float32)


def draw_audio_saved(key, part):
    base = shared_audio(key)
    values = jnp.clip(base, -4.0, 4.0)
    return values.astype(jnp.bfloat16)


def draw_video_saved(key, part):
    key = jax.random.fold_in(key, 5)
    fresh = jax.random.normal(key, (N_SECTION, MB, VID_TOKENS, D), jnp.float32)
    values = jnp.clip(fresh, -4.0, 4.0)
    return values.astype(jnp.bfloat16)


def window_draw(key):
    lower_key, upper_key = jax.random.split(key)
    shard = jnp.arange(N_SEQ, dtype=jnp.int32)
    lower = jax.random.randint(lower_key, (N_SEQ,), 0, 2, dtype=jnp.int32)
    upper = jax.random.randint(upper_key, (N_SEQ,), 0, 2, dtype=jnp.int32)
    start = jnp.maximum(4 * shard - 2 + lower, 0)
    finish = jnp.minimum(4 * shard + 6 - upper, 4 * N_SEQ)
    start = jnp.where(shard == 1, 2, start)
    finish = jnp.where(shard == 1, 10, finish)
    return jnp.stack([start, finish], axis=1).astype(jnp.int32)


def draw_video_window(key, part):
    key = jax.random.fold_in(key, 7)
    return window_draw(key)


def draw_audio_window(key, part):
    key = jax.random.fold_in(key, 9)
    return window_draw(key)


def levels(own_key, shape, cuts, least, high):
    level, own = 1.0, jax.random.fold_in(own_key, 6)
    for axis_at, parts in cuts:
        draws = jnp.exp(jax.random.uniform(jax.random.fold_in(own, axis_at), (parts,), jnp.float32, least / len(cuts), high / len(cuts)))
        level = level * jnp.repeat(draws, shape[axis_at] // parts).reshape([-1 if axis == axis_at else 1 for axis in range(len(shape))])
    return level


def normal_values(key, extent, scale, bound, shards=(), kind=jnp.bfloat16):
    array = scale * jax.random.normal(key, extent, jnp.float32)
    if shards:
        array = array * levels(key, extent, shards, -0.22, 0.18)
    return jnp.clip(array, -bound, bound).astype(kind)


def setup_inputs(seed: int = 0) -> dict:
    key_of = jax.random.split(jax.random.key(seed), 8)
    return {
        "video_saved": draw_video_saved(jax.random.fold_in(key_of[7], 71), 0),
        "audio_saved": draw_audio_saved(jax.random.fold_in(key_of[7], 71), 0),
        "video_cotangent": normal_values(key_of[2], (MB, VID_TOKENS, D), 1.0, 6.0, ((1, 64),)),
        "audio_cotangent": normal_values(key_of[3], (MB, AUD_TOKENS, D), 1.0, 6.0, ((1, 64),)),
        "modulation": jnp.clip(1.0 + 0.15 * jax.random.normal(key_of[4], (N_SECTION, 4, D), jnp.float32), 0.25, 1.75),
        "video_window": draw_video_window(jax.random.fold_in(key_of[7], 71), 0),
        "audio_window": draw_audio_window(jax.random.fold_in(key_of[7], 71), 0),
    }


precise = lax.Precision.HIGHEST

def window_mask(shard, shard_rows, block_rows, window):
    positions = shard * shard_rows - shard_rows // 2 + jnp.arange(2 * shard_rows, dtype=jnp.int32)
    blocks = jnp.floor_divide(positions, block_rows)
    return (blocks >= window[0]) & (blocks < window[1])

def cross_attend(queries, keys, values, allowed, head_size):
    count = queries.shape[0]
    width = queries.shape[1]
    heads = width // head_size
    query_heads = queries.reshape(count, heads, head_size)
    key_heads = keys.reshape(keys.shape[0], heads, head_size)
    value_heads = values.reshape(values.shape[0], heads, head_size)
    scores = jnp.einsum('qhd,khd->hqk', query_heads, key_heads, precision=precise) * head_size ** (-0.5)
    scores = jnp.where(allowed[None, None, :], scores, -1e+30)
    largest = lax.stop_gradient(lax.optimization_barrier(jnp.max(scores, axis=2, keepdims=True)))
    weights = jnp.exp(scores - largest)
    weights = weights / lax.optimization_barrier(jnp.sum(weights, axis=2, keepdims=True))
    mixed = jnp.einsum('hqk,khd->qhd', weights, value_heads, precision=precise)
    return mixed.reshape(count, width)

def block_layer(video_ext, audio_ext, mods, video_allowed, audio_allowed, head_size):
    video_count = video_ext.shape[0] // 2
    audio_count = audio_ext.shape[0] // 2
    video_own = video_ext[video_count // 2:video_count // 2 + video_count]
    audio_own = audio_ext[audio_count // 2:audio_count // 2 + audio_count]
    video_mixed = cross_attend(video_own, audio_ext * mods[0], audio_ext, video_allowed, head_size)
    audio_mixed = cross_attend(audio_own, video_ext * mods[1], video_ext, audio_allowed, head_size)
    return (video_own + mods[2] * video_mixed, audio_own + mods[3] * audio_mixed)

def reference(video_saved, audio_saved, video_cotangent, audio_cotangent, modulation, video_window, audio_window):

    def layer(video_full, audio_full, mods):
        video_pad = jnp.pad(video_full, ((VID_DEV // 2, VID_DEV // 2), (0, 0)))
        audio_pad = jnp.pad(audio_full, ((AUD_DEV // 2, AUD_DEV // 2), (0, 0)))

        def one_shard(shard):
            video_ext = lax.dynamic_slice_in_dim(video_pad, shard * VID_DEV, 2 * VID_DEV, 0)
            audio_ext = lax.dynamic_slice_in_dim(audio_pad, shard * AUD_DEV, 2 * AUD_DEV, 0)
            video_allowed = window_mask(shard, AUD_DEV, AUD_DEV // 4, video_window[shard])
            audio_allowed = window_mask(shard, VID_DEV, VID_DEV // 4, audio_window[shard])
            return block_layer(video_ext, audio_ext, mods, video_allowed, audio_allowed, HDIM)
        video_out, audio_out = lax.map(one_shard, jnp.arange(N_SEQ, dtype=jnp.int32))
        return (video_out.reshape(-1, D), audio_out.reshape(-1, D))
    video_down = video_cotangent
    audio_down = audio_cotangent
    video_layers = []
    audio_layers = []
    mod_layers = []
    for section in reversed(range(N_SECTION)):
        video_list = []
        audio_list = []
        mod_total = jnp.zeros((4, D), jnp.float32)
        for micro in range(MB):
            _, pull = jax.vjp(layer, video_saved[section, micro].astype(jnp.float32), audio_saved[section, micro].astype(jnp.float32), modulation[section].astype(jnp.float32))
            video_part, audio_part, mod_part = pull((video_down[micro].astype(jnp.float32), audio_down[micro].astype(jnp.float32)))
            video_list.append(video_part.astype(jnp.bfloat16))
            audio_list.append(audio_part.astype(jnp.bfloat16))
            mod_total = mod_total + mod_part
        video_down = jnp.stack(video_list)
        audio_down = jnp.stack(audio_list)
        video_layers.append(video_down)
        audio_layers.append(audio_down)
        mod_layers.append(mod_total)
    video_grad = jnp.stack(video_layers[::-1])
    audio_grad = jnp.stack(audio_layers[::-1])
    modulation_grad = jnp.stack(mod_layers[::-1])
    return (video_grad, audio_grad, modulation_grad)
```

```python
import functools

import jax
import jax.numpy as jnp
from jax import lax
from jax.experimental import pallas as pl
from jax.experimental.pallas import tpu as pltpu
from jax.sharding import PartitionSpec as P


HDIM = 128
MB = 2
VH = 32
AH = 16
GROUP = VH + AH
HALF = MB * GROUP
ROWS = 2 * HALF
MODS = 16
SCALE = HDIM**-0.5
LARGE = 60
OWN_LIMIT = 40
F32 = jnp.float32
BF16 = jnp.bfloat16
SMEM = pl.BlockSpec(memory_space=pltpu.SMEM)


def call(body, out_shape, flops=0, moved=1 << 20, limit=40, **kw):
    return pl.pallas_call(
        body,
        out_shape=out_shape,
        cost_estimate=pl.CostEstimate(flops=flops, bytes_accessed=moved, transcendentals=0),
        compiler_params=pltpu.CompilerParams(vmem_limit_bytes=limit << 20),
        **kw,
    )


def shape(*dims, dtype=BF16):
    return jax.ShapeDtypeStruct(dims, dtype)


def dot(a, b, dims):
    return lax.dot_general(a, b, (dims, ((), ())), preferred_element_type=F32)


def rows_of(half, seq):
    odd = seq % 2
    part = odd if half == 0 else 1 - odd
    v_rows = pl.ds(pl.multiple_of(part * VH, VH), VH)
    a_rows = pl.ds(pl.multiple_of(part * AH, AH), AH)
    return v_rows, a_rows


def section_order(count):
    return sorted(range(count), key=lambda k: (k == 0, min(k, count - k)))


def prepare(order, *refs):
    half_refs = (len(refs) - 1 - len(order) - (0 in order)) // 2
    inputs, outs, fetched, sems = (
        refs[:half_refs],
        refs[half_refs : -1 - half_refs],
        refs[-1 - half_refs : -1],
        refs[-1],
    )
    copies = [
        pltpu.make_async_copy(source, target, sems.at[i])
        for i, (source, target) in enumerate(zip(inputs, fetched))
    ]
    for copy in copies:
        copy.start()
    for copy in copies:
        copy.wait()
    video, audio, mods, v_window, a_window = fetched[:5]
    count, width = lax.axis_size("section"), outs[0].shape[1]
    section, seq = lax.axis_index("section"), lax.axis_index("seq")
    ends = [v_window[0, 0], v_window[0, 1], a_window[0, 0], a_window[0, 1]]
    ends = [jnp.full((1, width), end - 4 * seq, jnp.int32).astype(F32) for end in ends]
    ends = jnp.concatenate(ends, axis=0).astype(BF16)
    for k, piece in zip(order, outs):
        columns = pl.ds(pl.multiple_of(lax.rem(section + k, count) * width, 128), width)
        for half in range(2):
            v_rows, a_rows = rows_of(half, seq)
            for m in range(MB):
                base = half * HALF + m * GROUP
                piece[base : base + VH] = video[0, m, v_rows, columns]
                piece[base + VH : base + GROUP] = audio[0, m, a_rows, columns]
                if k == 0:
                    video_cot, audio_cot = fetched[5:]
                    outs[-1][base : base + VH] = video_cot[m, v_rows, columns]
                    outs[-1][base + VH : base + GROUP] = audio_cot[m, a_rows, columns]
        value = mods[0, :, columns]
        high = value.astype(BF16)
        rest = value - high.astype(F32)
        middle = rest.astype(BF16)
        low = (rest - middle.astype(F32)).astype(BF16)
        piece[ROWS : ROWS + MODS] = jnp.concatenate([high, middle, low, ends], axis=0)


def assemble(*refs):
    pieces, (far, near, extra) = refs[:-3], refs[-3:]
    count, section = len(pieces), lax.axis_index("section")
    for k, piece in zip(section_order(count), pieces):
        layer = lax.rem(section - k + count, count)
        far[layer] = piece[:HALF]
        near[layer] = piece[HALF:ROWS]
        extra[layer] = piece[ROWS : ROWS + MODS]


def read_mods(extra):
    parts = extra[0].astype(F32)
    return parts[0:4] + parts[4:8] + parts[8:12]


def contexts(data, m):
    far_own, near_own, far_in, near_in = data
    at = m * GROUP
    refs = (far_in, far_own, near_own, near_in)
    video = [ref[0, at : at + VH] for ref in refs]
    audio = [ref[0, at + VH : at + GROUP] for ref in refs]
    return jnp.concatenate(video, axis=0), jnp.concatenate(audio, axis=0)


def allowed_row(extra, at, count):
    ends = extra[0].astype(F32)[:, :count].astype(jnp.int32)
    row = lax.broadcasted_iota(jnp.int32, (1, count), 1)
    per_piece = count // 4
    piece = row // per_piece
    piece = jnp.where(lax.axis_index("seq") % 2 == 1, 3 - piece, piece)
    block = 2 * piece - 2 + (row % per_piece) // (per_piece // 2)
    return (block >= ends[at : at + 1]) & (block < ends[at + 1 : at + 2])


def masks(extra):
    return allowed_row(extra, 12, 4 * AH), allowed_row(extra, 14, 4 * VH)


def split(value):
    high = value.astype(BF16)
    return high, (value - high.astype(F32)).astype(BF16)


def dot_rows(parts, b, dims):
    count = parts[0].shape[0]
    both = dot(jnp.concatenate(parts, axis=0), b, dims)
    return both[:count] + both[count:]


def softmax_all(units):
    scores = []
    for queries, context, allowed in units:
        products = dot_rows(split(queries), context, ((1,), (1,)))
        scores.append(jnp.where(allowed, products, -1e30))
    largest = [jnp.max(x, axis=1, keepdims=True) for x in scores]
    weights = [jnp.exp(x - y) for x, y in zip(scores, largest)]
    sums = [jnp.sum(x, axis=1, keepdims=True) for x in weights]
    return [x / y for x, y in zip(weights, sums)]


def heads_of(width):
    return [(h, slice(h * HDIM, (h + 1) * HDIM)) for h in range(width // HDIM)]


def forward_layer(data, extra, store):
    width = extra.shape[2]
    mods = read_mods(extra)
    v_allowed, a_allowed = masks(extra)
    v_scale = mods[0:1] * SCALE
    a_scale = mods[1:2] * SCALE
    keys, units = [], []
    for m in range(MB):
        v_ctx, a_ctx = contexts(data, m)
        v_own = v_ctx[VH : 3 * VH].astype(F32) * v_scale
        a_own = a_ctx[AH : 3 * AH].astype(F32) * a_scale
        for h, cols in heads_of(width):
            keys += [(0, m, h), (1, m, h)]
            units.append((v_own[:, cols], a_ctx[:, cols], v_allowed))
            units.append((a_own[:, cols], v_ctx[:, cols], a_allowed))
    for key, weights in zip(keys, softmax_all(units)):
        store(*key, weights)


def attend_back(units):
    grads = [split(cot * gate) for _, cot, _, _, _, gate in units]
    by_weights = [dot_rows(g, unit[3], ((1,), (1,))) for g, unit in zip(grads, units)]
    products = [unit[0] * by for by, unit in zip(by_weights, units)]
    means = [jnp.sum(product, axis=1, keepdims=True) for product in products]
    boths = [
        split(jnp.concatenate([unit[0], unit[0] * (by - mean)], axis=0))
        for by, mean, unit in zip(by_weights, means, units)
    ]
    outs = [dot_rows(both, unit[3], ((1,), (0,))) for both, unit in zip(boths, units)]
    found = []
    for grad, both, out, (_, cot, own, _, scale, _) in zip(grads, boths, outs, units):
        count = cot.shape[0]
        own32 = own.astype(F32)
        scaled = split(own32 * scale)
        high, low = (jnp.concatenate([g, q], axis=0) for g, q in zip(grad, scaled))
        by_context = dot(
            jnp.concatenate([both[0], both[1], both[0]], axis=0),
            jnp.concatenate([high, high, low], axis=0),
            ((0,), (0,)),
        )
        mixed, back = out[:count], out[count:]
        by_scale = jnp.sum(own32 * back, axis=0, keepdims=True) * SCALE
        by_gate = jnp.sum(cot * mixed, axis=0, keepdims=True)
        found.append((back * scale, by_context, by_scale, by_gate))
    return found


def backward_layer(data, extra, cots, load, outs):
    width = extra.shape[2]
    mods = read_mods(extra)
    own_out, far_out, near_out = outs
    units, places = [], []
    for m in range(MB):
        v_all, a_all = contexts(data, m)
        for h, cols in heads_of(width):
            v_ctx, a_ctx = v_all[:, cols], a_all[:, cols]
            first, second = m * GROUP, HALF + m * GROUP
            v_cot = jnp.concatenate(
                [cots[first : first + VH, cols], cots[second : second + VH, cols]], axis=0
            )
            a_cot = jnp.concatenate(
                [
                    cots[first + VH : first + GROUP, cols],
                    cots[second + VH : second + GROUP, cols],
                ],
                axis=0,
            )
            v_scale, a_scale = mods[0:1, cols] * SCALE, mods[1:2, cols] * SCALE
            v_own, a_own = v_ctx[VH : 3 * VH], a_ctx[AH : 3 * AH]
            units.append((load(0, m, h), v_cot, v_own, a_ctx, v_scale, mods[2:3, cols]))
            units.append((load(1, m, h), a_cot, a_own, v_ctx, a_scale, mods[3:4, cols]))
            places.append((h, cols, first, second))
    found = attend_back(units)
    by_mods = {}
    for at, (h, cols, first, second) in enumerate(places):
        v_q, a_by, s0, g2 = found[2 * at]
        a_q, v_by, s1, g3 = found[2 * at + 1]
        rows = jnp.concatenate([s0, s1, g2, g3], axis=0)
        by_mods[h] = by_mods[h] + rows if h in by_mods else rows
        v_total = units[2 * at][1] + v_q + v_by[VH : 3 * VH]
        a_total = units[2 * at + 1][1] + a_q + a_by[AH : 3 * AH]
        own_out[first : first + VH, cols] = v_total[:VH]
        own_out[first + VH : first + GROUP, cols] = a_total[:AH]
        own_out[second : second + VH, cols] = v_total[VH:]
        own_out[second + VH : second + GROUP, cols] = a_total[AH:]
        far_out[first : first + VH, cols] = v_by[:VH].astype(BF16)
        far_out[first + VH : first + GROUP, cols] = a_by[:AH].astype(BF16)
        near_out[first : first + VH, cols] = v_by[3 * VH :].astype(BF16)
        near_out[first + VH : first + GROUP, cols] = a_by[3 * AH :].astype(BF16)
    return jnp.concatenate([by_mods[h] for h, _ in heads_of(width)], axis=1)


def top_layer(far_own, near_own, far_in, near_in, extra, cots, own_out, far_out, near_out, mods):
    found = {}

    def store(*key_value):
        found[key_value[:3]] = key_value[3]

    data = (far_own, near_own, far_in, near_in)
    forward_layer(data, extra, store)
    mods[...] = jnp.zeros_like(mods)
    mods[mods.shape[0] - 1] = backward_layer(
        data, extra, cots[...].astype(F32), lambda *key: found[key], (own_out, far_out, near_out)
    )


def weights_ahead(far_own, near_own, far_in, near_in, extra, v_weights, a_weights):
    def store(kind, m, h, value):
        (v_weights, a_weights)[kind][0, m, h] = value

    forward_layer((far_own, near_own, far_in, near_in), extra, store)


def joined(own, far_in, near_in):
    first = own[:HALF].astype(F32) + far_in[...].astype(F32)
    second = own[HALF:].astype(F32) + near_in[...].astype(F32)
    return jnp.concatenate([first, second], axis=0).astype(BF16)


def lower_layer(layer, *refs):
    data, extra, (own, far_part, near_part, v_weights, a_weights, mods_in) = (
        refs[:4],
        refs[4],
        refs[5:11],
    )
    total_out, mods, *outs = refs[11:16]
    total = joined(own, far_part, near_part)
    total_out[...] = total
    mods[...] = mods_in[...]
    mods[layer] = backward_layer(
        data,
        extra,
        total.astype(F32),
        lambda kind, m, h: (v_weights, a_weights)[kind][0, m, h],
        outs,
    )
    for spread in refs[16:]:
        copies = spread.shape[0] // mods.shape[0]
        for at in range(spread.shape[0]):
            spread[at] = mods[at // copies]


def group_sum(own, moved):
    total = own[...] + moved[0][...]
    return total + (moved[1][...] + moved[2][...]) if len(moved) == 3 else total


def gather_totals(own, far_part, near_part, *refs):
    totals, spread, out, mods = refs[:-3], *refs[-3:]
    out[0] = joined(own, far_part, near_part)
    for at, total in enumerate(totals):
        out[at + 1] = total[...]
    count = out.shape[0]
    copies = spread.shape[0] // count
    chunks = []
    for c in range(count):
        chunks.append(sum((spread[c * copies + i] for i in range(1, copies)), spread[c * copies]))
    mods[0] = jnp.concatenate(chunks, axis=1)


def add_group(own, *refs):
    refs[-1][...] = group_sum(own, refs[:-1])


def finish(received, mods, *refs):
    moved, (video, audio, mods_out) = refs[:-3], refs[-3:]
    mods_out[...] = group_sum(mods, moved)
    count, _, width = received.shape
    seq = lax.axis_index("seq")
    for chunk in range(count):
        columns = pl.ds(chunk * width, width)
        for half in range(2):
            v_rows, a_rows = rows_of(half, seq)
            for m in range(MB):
                base = half * HALF + m * GROUP
                video[0, m, v_rows, columns] = received[chunk, base : base + VH]
                audio[0, m, a_rows, columns] = received[chunk, base + VH : base + GROUP]


def swap(value, first):
    pairs = [(i, i + 1) for i in range(first, lax.axis_size("seq") - 1, 2)]
    return lax.ppermute(value, "seq", pairs + [(b, a) for a, b in pairs])


def swap_near(value):
    return swap(value, 0)


def swap_far(value):
    return swap(value, 1)


def to_section(value, k):
    count = lax.axis_size("section")
    if k == 0:
        return value
    return lax.ppermute(value, "section", [(s, (s + k) % count) for s in range(count)])


def split_bits(count):
    return ((0, 5), ((1, 2), (3, 4))) if count == 64 else ((0,), ((1,),))


def home_and_sum(spread):
    sections, count = lax.axis_size("section"), lax.axis_size("seq")
    bits = split_bits(count)[0]
    mask = sum(1 << bit for bit in bits)
    members = [i for i in range(count) if i & ~mask == 0]
    groups = [
        [s * count + base + i for s in range(sections) for i in members]
        for base in range(count)
        if base & mask == 0
    ]
    return lax.all_to_all(
        spread, ("section", "seq"), 0, 0, axis_index_groups=groups, tiled=True
    )


def group_moves(value, bits):
    count = lax.axis_size("seq")
    masks = [1 << bits[0]]
    if len(bits) == 2:
        masks += [1 << bits[1], 1 << bits[0] | 1 << bits[1]]
    return [lax.ppermute(value, "seq", [(i, i ^ mask) for i in range(count)]) for mask in masks]


def local(video_saved, audio_saved, video_cot, audio_cot, modulation, v_window, a_window):
    sections, count = lax.axis_size("section"), lax.axis_size("seq")
    width = video_saved.shape[3] // sections
    heads = width // HDIM
    flops = 200_000_000

    def whole(*dims):
        return pl.BlockSpec(dims, lambda *_: (0,) * len(dims))

    def like(arrays):
        return [whole(*a.shape) for a in arrays]

    def run(body, arrays, outs, specs=None, **kw):
        return call(
            body,
            tuple(outs),
            grid=(1,),
            in_specs=specs or like(arrays),
            out_specs=tuple(like(outs)),
            **kw,
        )(*arrays)

    hbm = pl.BlockSpec(memory_space=pltpu.HBM)

    def run_prepare(order, arrays, outs, limit):
        return call(
            functools.partial(prepare, order),
            outs,
            grid=(1,),
            in_specs=[hbm] * len(arrays),
            out_specs=tuple(like(outs)),
            limit=limit,
            scratch_shapes=[
                (pltpu.VMEM if a.size > 2 else pltpu.SMEM)(a.shape, a.dtype) for a in arrays
            ]
            + [pltpu.SemaphoreType.DMA((len(arrays),))],
            name="prepare" if order[0] else "prepare_own",
        )(*arrays)

    inputs = (video_saved, audio_saved, modulation, v_window, a_window)
    piece = shape(ROWS + MODS, width)
    order = section_order(sections)
    sent = run_prepare(order[:-1], inputs, (piece,) * (sections - 1), LARGE)
    pieces = [to_section(value, k) for value, k in zip(sent, order)]
    own_piece, cots = run_prepare(
        order[-1:], inputs + (video_cot, audio_cot), (piece, shape(ROWS, width)), OWN_LIMIT
    )
    pieces.append(own_piece)
    far_own, near_own, extra = run(
        assemble,
        tuple(pieces),
        [shape(sections, HALF, width), shape(sections, HALF, width), shape(sections, MODS, width)],
        name="assemble",
    )
    far_in = swap_far(far_own)
    near_in = swap_near(near_own)
    data = (far_own, near_own, far_in, near_in, extra)

    def layer_specs(index):
        return [pl.BlockSpec((1,) + a.shape[1:], lambda *i: (index(*i), 0, 0)) for a in data]

    chain = [
        shape(ROWS, width, dtype=F32),
        shape(HALF, width),
        shape(HALF, width),
        shape(sections, 4, width, dtype=F32),
    ]
    top = sections - 1
    own, far_out, near_out, mods = run(
        top_layer,
        data + (cots,),
        chain,
        layer_specs(lambda *_: top) + like([cots]),
        flops=flops,
        name="top_layer",
    )
    blocks = [(1, MB, heads, 2 * VH, 4 * AH), (1, MB, heads, 2 * AH, 4 * VH)]
    weights = call(
        weights_ahead,
        tuple(shape(top, *block[1:], dtype=F32) for block in blocks),
        flops=3 * flops,
        grid=(top,),
        in_specs=layer_specs(lambda i: i),
        out_specs=tuple(pl.BlockSpec(block, lambda i: (i, 0, 0, 0, 0)) for block in blocks),
        name="weights_ahead",
    )(*data)

    home_bits, steps = split_bits(count)
    spread_shape = shape(sections << len(home_bits), 4, width, dtype=F32)
    totals = []
    part = (own, swap_far(far_out), swap_near(near_out))
    for layer in reversed(range(top)):
        weight_specs = [pl.BlockSpec(b, lambda *_, at=layer: (at, 0, 0, 0, 0)) for b in blocks]
        total, mods, own, far_out, near_out, *spread = run(
            functools.partial(lower_layer, layer),
            data + part + tuple(weights) + (mods,),
            [shape(ROWS, width), chain[3]] + chain[:3] + ([] if layer else [spread_shape]),
            layer_specs(lambda *_, at=layer: at) + like(part) + weight_specs + like([mods]),
            flops=flops,
            name="lower_layer",
        )
        part = (own, swap_far(far_out), swap_near(near_out))
        totals.append(total)

    mods_shape = shape(1, 4, sections * width, dtype=F32)
    out, mods = run(
        gather_totals,
        part + tuple(reversed(totals)) + (home_and_sum(spread[0]),),
        [shape(sections, ROWS, width), mods_shape],
        name="gather_totals",
    )
    received = lax.all_to_all(out, "section", 0, 0, tiled=True)
    for bits in steps[:-1]:
        (mods,) = run(add_group, (mods, *group_moves(mods, bits)), [mods_shape], name="add_group")
    return tuple(
        run(
            finish,
            (received, mods, *group_moves(mods, steps[-1])),
            [shape(*video_saved.shape), shape(*audio_saved.shape), mods_shape],
            name="finish",
        )
    )


def solution(mesh):
    return jax.shard_map(
        local,
        mesh=mesh,
        in_specs=(
            P("section", None, "seq", None),
            P("section", None, "seq", None),
            P(None, "seq", None),
            P(None, "seq", None),
            P("section", None, None),
            P("seq", None),
            P("seq", None),
        ),
        out_specs=(
            P("section", None, "seq", None),
            P("section", None, "seq", None),
            P("section", None, None),
        ),
        check_vma=False,
    )
```

```python
import functools

import jax
import jax.numpy as jnp
from jax import lax
from jax.experimental import pallas as pl
from jax.experimental.pallas import tpu as pltpu
from jax.sharding import PartitionSpec as P


HDIM = 128
MB = 2
VH = 32
AH = 16
GROUP = VH + AH
HALF = MB * GROUP
ROWS = 2 * HALF
MODS = 16
SCALE = HDIM**-0.5
LARGE = 60
OWN_LIMIT = 40
F32 = jnp.float32
BF16 = jnp.bfloat16
SMEM = pl.BlockSpec(memory_space=pltpu.SMEM)


def call(body, out_shape, flops=0, moved=1 << 20, limit=40, **kw):
    return pl.pallas_call(
        body,
        out_shape=out_shape,
        cost_estimate=pl.CostEstimate(flops=flops, bytes_accessed=moved, transcendentals=0),
        compiler_params=pltpu.CompilerParams(vmem_limit_bytes=limit << 20),
        **kw,
    )


def shape(*dims, dtype=BF16):
    return jax.ShapeDtypeStruct(dims, dtype)


def dot(a, b, dims):
    return lax.dot_general(a, b, (dims, ((), ())), preferred_element_type=F32)


def rows_of(half, seq):
    odd = seq % 2
    part = odd if half == 0 else 1 - odd
    v_rows = pl.ds(pl.multiple_of(part * VH, VH), VH)
    a_rows = pl.ds(pl.multiple_of(part * AH, AH), AH)
    return v_rows, a_rows


def section_order(count):
    return sorted(range(count), key=lambda k: (k == 0, min(k, count - k)))


def prepare(order, *refs):
    half_refs = (len(refs) - 1 - len(order) - (0 in order)) // 2
    inputs, outs, fetched, sems = (
        refs[:half_refs],
        refs[half_refs : -1 - half_refs],
        refs[-1 - half_refs : -1],
        refs[-1],
    )
    copies = [
        pltpu.make_async_copy(source, target, sems.at[i])
        for i, (source, target) in enumerate(zip(inputs, fetched))
    ]
    for copy in copies:
        copy.start()
    for copy in copies:
        copy.wait()
    video, audio, mods, v_window, a_window = fetched[:5]
    count, width = lax.axis_size("section"), outs[0].shape[1]
    section, seq = lax.axis_index("section"), lax.axis_index("seq")
    ends = [v_window[0, 0], v_window[0, 1], a_window[0, 0], a_window[0, 1]]
    ends = [jnp.full((1, width), end - 4 * seq, jnp.int32).astype(F32) for end in ends]
    ends = jnp.concatenate(ends, axis=0).astype(BF16)
    for k, piece in zip(order, outs):
        columns = pl.ds(pl.multiple_of(lax.rem(section + k, count) * width, 128), width)
        for half in range(2):
            v_rows, a_rows = rows_of(half, seq)
            for m in range(MB):
                base = half * HALF + m * GROUP
                piece[base : base + VH] = video[0, m, v_rows, columns]
                piece[base + VH : base + GROUP] = audio[0, m, a_rows, columns]
                if k == 0:
                    video_cot, audio_cot = fetched[5:]
                    outs[-1][base : base + VH] = video_cot[m, v_rows, columns]
                    outs[-1][base + VH : base + GROUP] = audio_cot[m, a_rows, columns]
        value = mods[0, :, columns]
        high = value.astype(BF16)
        rest = value - high.astype(F32)
        middle = rest.astype(BF16)
        low = (rest - middle.astype(F32)).astype(BF16)
        piece[ROWS : ROWS + MODS] = jnp.concatenate([high, middle, low, ends], axis=0)


def assemble(*refs):
    pieces, (far, near, extra) = refs[:-3], refs[-3:]
    count, section = len(pieces), lax.axis_index("section")
    for k, piece in zip(section_order(count), pieces):
        layer = lax.rem(section - k + count, count)
        far[layer] = piece[:HALF]
        near[layer] = piece[HALF:ROWS]
        extra[layer] = piece[ROWS : ROWS + MODS]


def read_mods(extra):
    parts = extra[0].astype(F32)
    return parts[0:4] + parts[4:8] + parts[8:12]


def contexts(data, m):
    far_own, near_own, far_in, near_in = data
    at = m * GROUP
    refs = (far_in, far_own, near_own, near_in)
    video = [ref[0, at : at + VH] for ref in refs]
    audio = [ref[0, at + VH : at + GROUP] for ref in refs]
    return jnp.concatenate(video, axis=0), jnp.concatenate(audio, axis=0)


def allowed_row(extra, at, count):
    ends = extra[0].astype(F32)[:, :count].astype(jnp.int32)
    row = lax.broadcasted_iota(jnp.int32, (1, count), 1)
    per_piece = count // 4
    piece = row // per_piece
    piece = jnp.where(lax.axis_index("seq") % 2 == 1, 3 - piece, piece)
    block = 2 * piece - 2 + (row % per_piece) // (per_piece // 2)
    return (block >= ends[at : at + 1]) & (block < ends[at + 1 : at + 2])


def masks(extra):
    return allowed_row(extra, 12, 4 * AH), allowed_row(extra, 14, 4 * VH)


def split(value):
    high = value.astype(BF16)
    return high, (value - high.astype(F32)).astype(BF16)


def dot_rows(parts, b, dims):
    count = parts[0].shape[0]
    both = dot(jnp.concatenate(parts, axis=0), b, dims)
    return both[:count] + both[count:]


def softmax_all(units):
    scores = []
    for queries, context, allowed in units:
        products = dot_rows(split(queries), context, ((1,), (1,)))
        scores.append(jnp.where(allowed, products, -1e30))
    largest = [jnp.max(x, axis=1, keepdims=True) for x in scores]
    weights = [jnp.exp(x - y) for x, y in zip(scores, largest)]
    sums = [jnp.sum(x, axis=1, keepdims=True) for x in weights]
    return [x / y for x, y in zip(weights, sums)]


def heads_of(width):
    return [(h, slice(h * HDIM, (h + 1) * HDIM)) for h in range(width // HDIM)]


def forward_layer(data, extra, store):
    width = extra.shape[2]
    mods = read_mods(extra)
    v_allowed, a_allowed = masks(extra)
    v_scale = mods[0:1] * SCALE
    a_scale = mods[1:2] * SCALE
    keys, units = [], []
    for m in range(MB):
        v_ctx, a_ctx = contexts(data, m)
        v_own = v_ctx[VH : 3 * VH].astype(F32) * v_scale
        a_own = a_ctx[AH : 3 * AH].astype(F32) * a_scale
        for h, cols in heads_of(width):
            keys += [(0, m, h), (1, m, h)]
            units.append((v_own[:, cols], a_ctx[:, cols], v_allowed))
            units.append((a_own[:, cols], v_ctx[:, cols], a_allowed))
    for key, weights in zip(keys, softmax_all(units)):
        store(*key, weights)


def attend_back(units):
    grads = [split(cot * gate) for _, cot, _, _, _, gate in units]
    by_weights = [dot_rows(g, unit[3], ((1,), (1,))) for g, unit in zip(grads, units)]
    products = [unit[0] * by for by, unit in zip(by_weights, units)]
    means = [jnp.sum(product, axis=1, keepdims=True) for product in products]
    boths = [
        split(jnp.concatenate([unit[0], unit[0] * (by - mean)], axis=0))
        for by, mean, unit in zip(by_weights, means, units)
    ]
    outs = [dot_rows(both, unit[3], ((1,), (0,))) for both, unit in zip(boths, units)]
    found = []
    for grad, both, out, (_, cot, own, _, scale, _) in zip(grads, boths, outs, units):
        count = cot.shape[0]
        own32 = own.astype(F32)
        scaled = split(own32 * scale)
        high, low = (jnp.concatenate([g, q], axis=0) for g, q in zip(grad, scaled))
        by_context = dot(
            jnp.concatenate([both[0], both[1], both[0]], axis=0),
            jnp.concatenate([high, high, low], axis=0),
            ((0,), (0,)),
        )
        mixed, back = out[:count], out[count:]
        by_scale = jnp.sum(own32 * back, axis=0, keepdims=True) * SCALE
        by_gate = jnp.sum(cot * mixed, axis=0, keepdims=True)
        found.append((back * scale, by_context, by_scale, by_gate))
    return found


def backward_layer(data, extra, cots, load, outs):
    width = extra.shape[2]
    mods = read_mods(extra)
    own_out, far_out, near_out = outs
    units, places = [], []
    for m in range(MB):
        v_all, a_all = contexts(data, m)
        for h, cols in heads_of(width):
            v_ctx, a_ctx = v_all[:, cols], a_all[:, cols]
            first, second = m * GROUP, HALF + m * GROUP
            v_cot = jnp.concatenate(
                [cots[first : first + VH, cols], cots[second : second + VH, cols]], axis=0
            )
            a_cot = jnp.concatenate(
                [
                    cots[first + VH : first + GROUP, cols],
                    cots[second + VH : second + GROUP, cols],
                ],
                axis=0,
            )
            v_scale, a_scale = mods[0:1, cols] * SCALE, mods[1:2, cols] * SCALE
            v_own, a_own = v_ctx[VH : 3 * VH], a_ctx[AH : 3 * AH]
            units.append((load(0, m, h), v_cot, v_own, a_ctx, v_scale, mods[2:3, cols]))
            units.append((load(1, m, h), a_cot, a_own, v_ctx, a_scale, mods[3:4, cols]))
            places.append((h, cols, first, second))
    found = attend_back(units)
    by_mods = {}
    for at, (h, cols, first, second) in enumerate(places):
        v_q, a_by, s0, g2 = found[2 * at]
        a_q, v_by, s1, g3 = found[2 * at + 1]
        rows = jnp.concatenate([s0, s1, g2, g3], axis=0)
        by_mods[h] = by_mods[h] + rows if h in by_mods else rows
        v_total = units[2 * at][1] + v_q + v_by[VH : 3 * VH]
        a_total = units[2 * at + 1][1] + a_q + a_by[AH : 3 * AH]
        own_out[first : first + VH, cols] = v_total[:VH]
        own_out[first + VH : first + GROUP, cols] = a_total[:AH]
        own_out[second : second + VH, cols] = v_total[VH:]
        own_out[second + VH : second + GROUP, cols] = a_total[AH:]
        far_out[first : first + VH, cols] = v_by[:VH].astype(BF16)
        far_out[first + VH : first + GROUP, cols] = a_by[:AH].astype(BF16)
        near_out[first : first + VH, cols] = v_by[3 * VH :].astype(BF16)
        near_out[first + VH : first + GROUP, cols] = a_by[3 * AH :].astype(BF16)
    return jnp.concatenate([by_mods[h] for h, _ in heads_of(width)], axis=1)


def top_layer(far_own, near_own, far_in, near_in, extra, cots, own_out, far_out, near_out, mods):
    found = {}

    def store(*key_value):
        found[key_value[:3]] = key_value[3]

    data = (far_own, near_own, far_in, near_in)
    forward_layer(data, extra, store)
    mods[...] = jnp.zeros_like(mods)
    mods[mods.shape[0] - 1] = backward_layer(
        data, extra, cots[...].astype(F32), lambda *key: found[key], (own_out, far_out, near_out)
    )


def weights_ahead(far_own, near_own, far_in, near_in, extra, v_weights, a_weights):
    def store(kind, m, h, value):
        (v_weights, a_weights)[kind][0, m, h] = value

    forward_layer((far_own, near_own, far_in, near_in), extra, store)


def joined(own, far_in, near_in):
    first = own[:HALF].astype(F32) + far_in[...].astype(F32)
    second = own[HALF:].astype(F32) + near_in[...].astype(F32)
    return jnp.concatenate([first, second], axis=0).astype(BF16)


def lower_layer(layer, *refs):
    data, extra, (own, far_part, near_part, v_weights, a_weights, mods_in) = (
        refs[:4],
        refs[4],
        refs[5:11],
    )
    total_out, mods, *outs = refs[11:]
    total = joined(own, far_part, near_part)
    total_out[...] = total
    mods[...] = mods_in[...]
    mods[layer] = backward_layer(
        data,
        extra,
        total.astype(F32),
        lambda kind, m, h: (v_weights, a_weights)[kind][0, m, h],
        outs,
    )


def ahead(mods, *refs):
    totals, (home, spread) = refs[:-2], refs[-2:]
    count = home.shape[0]
    for at, total in enumerate(totals):
        home[count - 1 - at] = total[...]
    copies = spread.shape[0] // count
    for at in range(spread.shape[0]):
        spread[at] = mods[at // copies]


def last_layer(*refs):
    data, extra, (own, far_part, near_part, v_weights, a_weights) = refs[:4], refs[4], refs[5:10]
    home, spread, *outs = refs[12:]
    total = joined(own, far_part, near_part)
    home[0] = total
    found = backward_layer(
        data,
        extra,
        total.astype(F32),
        lambda kind, m, h: (v_weights, a_weights)[kind][0, m, h],
        outs,
    )
    for at in range(spread.shape[0]):
        spread[at] = found


def group_sum(own, moved):
    total = own[...] + moved[0][...]
    return total + (moved[1][...] + moved[2][...]) if len(moved) == 3 else total


def gather_totals(own, far_part, near_part, _, spread, out, mods):
    out[0] = joined(own, far_part, near_part)
    count = mods.shape[2] // own.shape[1]
    copies = spread.shape[0] // count
    chunks = []
    for c in range(count):
        chunks.append(sum((spread[c * copies + i] for i in range(1, copies)), spread[c * copies]))
    mods[0] = jnp.concatenate(chunks, axis=1)


def add_group(own, *refs):
    refs[-1][...] = group_sum(own, refs[:-1])


def finish(received, mods, *refs):
    moved, (video, audio, mods_out) = refs[:-3], refs[-3:]
    mods_out[...] = group_sum(mods, moved)
    count, _, width = received.shape
    seq = lax.axis_index("seq")
    for chunk in range(count):
        columns = pl.ds(chunk * width, width)
        for half in range(2):
            v_rows, a_rows = rows_of(half, seq)
            for m in range(MB):
                base = half * HALF + m * GROUP
                video[0, m, v_rows, columns] = received[chunk, base : base + VH]
                audio[0, m, a_rows, columns] = received[chunk, base + VH : base + GROUP]


def swap(value, first):
    pairs = [(i, i + 1) for i in range(first, lax.axis_size("seq") - 1, 2)]
    return lax.ppermute(value, "seq", pairs + [(b, a) for a, b in pairs])


def swap_near(value):
    return swap(value, 0)


def swap_far(value):
    return swap(value, 1)


def to_section(value, k):
    count = lax.axis_size("section")
    if k == 0:
        return value
    return lax.ppermute(value, "section", [(s, (s + k) % count) for s in range(count)])


def split_bits(count):
    return ((0, 5), ((1, 2), (3, 4))) if count == 64 else ((0,), ((1,),))


def home_and_sum(spread):
    sections, count = lax.axis_size("section"), lax.axis_size("seq")
    bits = split_bits(count)[0]
    mask = sum(1 << bit for bit in bits)
    members = [i for i in range(count) if i & ~mask == 0]
    groups = [
        [s * count + base + i for s in range(sections) for i in members]
        for base in range(count)
        if base & mask == 0
    ]
    return lax.all_to_all(
        spread, ("section", "seq"), 0, 0, axis_index_groups=groups, tiled=True
    )


def group_moves(value, bits):
    count = lax.axis_size("seq")
    masks = [1 << bits[0]]
    if len(bits) == 2:
        masks += [1 << bits[1], 1 << bits[0] | 1 << bits[1]]
    return [lax.ppermute(value, "seq", [(i, i ^ mask) for i in range(count)]) for mask in masks]


def local(video_saved, audio_saved, video_cot, audio_cot, modulation, v_window, a_window):
    sections, count = lax.axis_size("section"), lax.axis_size("seq")
    width = video_saved.shape[3] // sections
    heads = width // HDIM
    flops = 200_000_000

    def whole(*dims):
        return pl.BlockSpec(dims, lambda *_: (0,) * len(dims))

    def like(arrays):
        return [whole(*a.shape) for a in arrays]

    def run(body, arrays, outs, specs=None, **kw):
        return call(
            body,
            tuple(outs),
            grid=(1,),
            in_specs=specs or like(arrays),
            out_specs=tuple(like(outs)),
            **kw,
        )(*arrays)

    hbm = pl.BlockSpec(memory_space=pltpu.HBM)

    def run_prepare(order, arrays, outs, limit):
        return call(
            functools.partial(prepare, order),
            outs,
            grid=(1,),
            in_specs=[hbm] * len(arrays),
            out_specs=tuple(like(outs)),
            limit=limit,
            scratch_shapes=[
                (pltpu.VMEM if a.size > 2 else pltpu.SMEM)(a.shape, a.dtype) for a in arrays
            ]
            + [pltpu.SemaphoreType.DMA((len(arrays),))],
            name="prepare" if order[0] else "prepare_own",
        )(*arrays)

    inputs = (video_saved, audio_saved, modulation, v_window, a_window)
    piece = shape(ROWS + MODS, width)
    order = section_order(sections)
    sent = run_prepare(order[:-1], inputs, (piece,) * (sections - 1), LARGE)
    pieces = [to_section(value, k) for value, k in zip(sent, order)]
    own_piece, cots = run_prepare(
        order[-1:], inputs + (video_cot, audio_cot), (piece, shape(ROWS, width)), OWN_LIMIT
    )
    pieces.append(own_piece)
    far_own, near_own, extra = run(
        assemble,
        tuple(pieces),
        [shape(sections, HALF, width), shape(sections, HALF, width), shape(sections, MODS, width)],
        name="assemble",
    )
    far_in = swap_far(far_own)
    near_in = swap_near(near_own)
    data = (far_own, near_own, far_in, near_in, extra)

    def layer_specs(index):
        return [pl.BlockSpec((1,) + a.shape[1:], lambda *i: (index(*i), 0, 0)) for a in data]

    chain = [
        shape(ROWS, width, dtype=F32),
        shape(HALF, width),
        shape(HALF, width),
        shape(sections, 4, width, dtype=F32),
    ]
    top = sections - 1
    own, far_out, near_out, mods = run(
        top_layer,
        data + (cots,),
        chain,
        layer_specs(lambda *_: top) + like([cots]),
        flops=flops,
        name="top_layer",
    )
    blocks = [(1, MB, heads, 2 * VH, 4 * AH), (1, MB, heads, 2 * AH, 4 * VH)]
    weights = call(
        weights_ahead,
        tuple(shape(top, *block[1:], dtype=F32) for block in blocks),
        flops=3 * flops,
        grid=(top,),
        in_specs=layer_specs(lambda i: i),
        out_specs=tuple(pl.BlockSpec(block, lambda i: (i, 0, 0, 0, 0)) for block in blocks),
        name="weights_ahead",
    )(*data)

    home_bits, steps = split_bits(count)
    spread_shape = shape(sections << len(home_bits), 4, width, dtype=F32)
    anywhere = pl.BlockSpec(memory_space=pl.ANY)
    home_shape = shape(sections, ROWS, width)

    def slot(at):
        return pl.BlockSpec((1, ROWS, width), lambda *_: (at, 0, 0))

    totals = []
    part = (own, swap_far(far_out), swap_near(near_out))
    for layer in reversed(range(top)):
        weight_specs = [pl.BlockSpec(b, lambda *_, at=layer: (at, 0, 0, 0, 0)) for b in blocks]
        specs = layer_specs(lambda *_, at=layer: at) + like(part) + weight_specs
        if layer:
            total, mods, own, far_out, near_out = run(
                functools.partial(lower_layer, layer),
                data + part + tuple(weights) + (mods,),
                [shape(ROWS, width), chain[3]] + chain[:3],
                specs + like([mods]),
                flops=flops,
                name="lower_layer",
            )
            totals.append(total)
        else:
            home, spread = run(
                ahead, (mods, *totals), [home_shape, spread_shape], name="ahead"
            )
            home, spread, own, far_out, near_out = call(
                last_layer,
                (home_shape, spread_shape, *chain[:3]),
                flops=flops,
                grid=(1,),
                in_specs=specs + [anywhere] * 2,
                out_specs=(slot(1), whole(1 << len(home_bits), 4, width), *like(chain[:3])),
                input_output_aliases={10: 0, 11: 1},
                name="last_layer",
            )(*data, *part, *weights, home, spread)
        part = (own, swap_far(far_out), swap_near(near_out))

    mods_shape = shape(1, 4, sections * width, dtype=F32)
    out, mods = call(
        gather_totals,
        (home_shape, mods_shape),
        grid=(1,),
        in_specs=like(part) + [anywhere] + like([spread_shape]),
        out_specs=(slot(0), *like([mods_shape])),
        input_output_aliases={3: 0},
        name="gather_totals",
    )(*part, home, home_and_sum(spread))
    received = lax.all_to_all(out, "section", 0, 0, tiled=True)
    for bits in steps[:-1]:
        (mods,) = run(add_group, (mods, *group_moves(mods, bits)), [mods_shape], name="add_group")
    return tuple(
        run(
            finish,
            (received, mods, *group_moves(mods, steps[-1])),
            [shape(*video_saved.shape), shape(*audio_saved.shape), mods_shape],
            name="finish",
        )
    )


def solution(mesh):
    return jax.shard_map(
        local,
        mesh=mesh,
        in_specs=(
            P("section", None, "seq", None),
            P("section", None, "seq", None),
            P(None, "seq", None),
            P(None, "seq", None),
            P("section", None, None),
            P("seq", None),
            P("seq", None),
        ),
        out_specs=(
            P("section", None, "seq", None),
            P("section", None, "seq", None),
            P("section", None, None),
        ),
        check_vma=False,
    )
```

```python
import functools

import jax
import jax.numpy as jnp
from jax import lax
from jax.experimental import pallas as pl
from jax.experimental.pallas import tpu as pltpu
from jax.sharding import PartitionSpec as P


HDIM = 128
MB = 2
VH = 32
AH = 16
GROUP = VH + AH
HALF = MB * GROUP
ROWS = 2 * HALF
MODS = 16
SCALE = HDIM**-0.5
LARGE = 60
OWN_LIMIT = 40
F32 = jnp.float32
BF16 = jnp.bfloat16
SMEM = pl.BlockSpec(memory_space=pltpu.SMEM)


def call(body, out_shape, flops=0, moved=1 << 20, limit=40, **kw):
    return pl.pallas_call(
        body,
        out_shape=out_shape,
        cost_estimate=pl.CostEstimate(flops=flops, bytes_accessed=moved, transcendentals=0),
        compiler_params=pltpu.CompilerParams(vmem_limit_bytes=limit << 20),
        **kw,
    )


def shape(*dims, dtype=BF16):
    return jax.ShapeDtypeStruct(dims, dtype)


def dot(a, b, dims):
    return lax.dot_general(a, b, (dims, ((), ())), preferred_element_type=F32)


def rows_of(half, seq):
    odd = seq % 2
    part = odd if half == 0 else 1 - odd
    v_rows = pl.ds(pl.multiple_of(part * VH, VH), VH)
    a_rows = pl.ds(pl.multiple_of(part * AH, AH), AH)
    return v_rows, a_rows


def section_order(count):
    return sorted(range(count), key=lambda k: (k == 0, min(k, count - k)))


def prepare(order, *refs):
    half_refs = (len(refs) - 1 - len(order) - (0 in order)) // 2
    inputs, outs, fetched, sems = (
        refs[:half_refs],
        refs[half_refs : -1 - half_refs],
        refs[-1 - half_refs : -1],
        refs[-1],
    )
    copies = [
        pltpu.make_async_copy(source, target, sems.at[i])
        for i, (source, target) in enumerate(zip(inputs, fetched))
    ]
    for copy in copies:
        copy.start()
    for copy in copies:
        copy.wait()
    video, audio, mods, v_window, a_window = fetched[:5]
    count, width = lax.axis_size("section"), outs[0].shape[1]
    section, seq = lax.axis_index("section"), lax.axis_index("seq")
    ends = [v_window[0, 0], v_window[0, 1], a_window[0, 0], a_window[0, 1]]
    ends = [jnp.full((1, width), end - 4 * seq, jnp.int32).astype(F32) for end in ends]
    ends = jnp.concatenate(ends, axis=0).astype(BF16)
    for k, piece in zip(order, outs):
        columns = pl.ds(pl.multiple_of(lax.rem(section + k, count) * width, 128), width)
        for half in range(2):
            v_rows, a_rows = rows_of(half, seq)
            for m in range(MB):
                base = half * HALF + m * GROUP
                piece[base : base + VH] = video[0, m, v_rows, columns]
                piece[base + VH : base + GROUP] = audio[0, m, a_rows, columns]
                if k == 0:
                    video_cot, audio_cot = fetched[5:]
                    outs[-1][base : base + VH] = video_cot[m, v_rows, columns]
                    outs[-1][base + VH : base + GROUP] = audio_cot[m, a_rows, columns]
        value = mods[0, :, columns]
        high = value.astype(BF16)
        rest = value - high.astype(F32)
        middle = rest.astype(BF16)
        low = (rest - middle.astype(F32)).astype(BF16)
        piece[ROWS : ROWS + MODS] = jnp.concatenate([high, middle, low, ends], axis=0)


def assemble(*refs):
    pieces, (far, near, extra) = refs[:-3], refs[-3:]
    count, section = len(pieces), lax.axis_index("section")
    for k, piece in zip(section_order(count), pieces):
        layer = lax.rem(section - k + count, count)
        far[layer] = piece[:HALF]
        near[layer] = piece[HALF:ROWS]
        extra[layer] = piece[ROWS : ROWS + MODS]


def read_mods(extra):
    parts = extra[0].astype(F32)
    return parts[0:4] + parts[4:8] + parts[8:12]


def contexts(data, m):
    far_own, near_own, far_in, near_in = data
    at = m * GROUP
    refs = (far_in, far_own, near_own, near_in)
    video = [ref[0, at : at + VH] for ref in refs]
    audio = [ref[0, at + VH : at + GROUP] for ref in refs]
    return jnp.concatenate(video, axis=0), jnp.concatenate(audio, axis=0)


def allowed_row(extra, at, count):
    ends = extra[0].astype(F32)[:, :count].astype(jnp.int32)
    row = lax.broadcasted_iota(jnp.int32, (1, count), 1)
    per_piece = count // 4
    piece = row // per_piece
    piece = jnp.where(lax.axis_index("seq") % 2 == 1, 3 - piece, piece)
    block = 2 * piece - 2 + (row % per_piece) // (per_piece // 2)
    return (block >= ends[at : at + 1]) & (block < ends[at + 1 : at + 2])


def masks(extra):
    return allowed_row(extra, 12, 4 * AH), allowed_row(extra, 14, 4 * VH)


def split(value):
    high = value.astype(BF16)
    return high, (value - high.astype(F32)).astype(BF16)


def dot_rows(parts, b, dims):
    count = parts[0].shape[0]
    both = dot(jnp.concatenate(parts, axis=0), b, dims)
    return both[:count] + both[count:]


def softmax_all(units):
    scores = []
    for queries, context, allowed in units:
        products = dot_rows(split(queries), context, ((1,), (1,)))
        scores.append(jnp.where(allowed, products, -1e30))
    largest = [jnp.max(x, axis=1, keepdims=True) for x in scores]
    weights = [jnp.exp(x - y) for x, y in zip(scores, largest)]
    sums = [jnp.sum(x, axis=1, keepdims=True) for x in weights]
    return [x / y for x, y in zip(weights, sums)]


def heads_of(width):
    return [(h, slice(h * HDIM, (h + 1) * HDIM)) for h in range(width // HDIM)]


def forward_layer(data, extra, store):
    width = extra.shape[2]
    mods = read_mods(extra)
    v_allowed, a_allowed = masks(extra)
    v_scale = mods[0:1] * SCALE
    a_scale = mods[1:2] * SCALE
    keys, units = [], []
    for m in range(MB):
        v_ctx, a_ctx = contexts(data, m)
        v_own = v_ctx[VH : 3 * VH].astype(F32) * v_scale
        a_own = a_ctx[AH : 3 * AH].astype(F32) * a_scale
        for h, cols in heads_of(width):
            keys += [(0, m, h), (1, m, h)]
            units.append((v_own[:, cols], a_ctx[:, cols], v_allowed))
            units.append((a_own[:, cols], v_ctx[:, cols], a_allowed))
    for key, weights in zip(keys, softmax_all(units)):
        store(*key, weights)


def attend_back(units):
    grads = [split(cot * gate) for _, cot, _, _, _, gate in units]
    by_weights = [dot_rows(g, unit[3], ((1,), (1,))) for g, unit in zip(grads, units)]
    products = [unit[0] * by for by, unit in zip(by_weights, units)]
    means = [jnp.sum(product, axis=1, keepdims=True) for product in products]
    boths = [
        split(jnp.concatenate([unit[0], unit[0] * (by - mean)], axis=0))
        for by, mean, unit in zip(by_weights, means, units)
    ]
    outs = []
    for (high, low), unit in zip(boths, units):
        count = unit[1].shape[0]
        out = dot(jnp.concatenate([high, low[count:]], axis=0), unit[3], ((1,), (0,)))
        outs.append((out[:count], out[count : 2 * count] + out[2 * count :]))
    found = []
    for grad, both, out, (_, cot, own, _, scale, _) in zip(grads, boths, outs, units):
        own32 = own.astype(F32)
        scaled = split(own32 * scale)
        high, low = (jnp.concatenate([g, q], axis=0) for g, q in zip(grad, scaled))
        by_context = dot(
            jnp.concatenate([both[0], both[1], both[0]], axis=0),
            jnp.concatenate([high, high, low], axis=0),
            ((0,), (0,)),
        )
        mixed, back = out
        by_scale = jnp.sum(own32 * back, axis=0, keepdims=True) * SCALE
        by_gate = jnp.sum(cot * mixed, axis=0, keepdims=True)
        found.append((back * scale, by_context, by_scale, by_gate))
    return found


def backward_layer(data, extra, cots, load, outs):
    width = extra.shape[2]
    mods = read_mods(extra)
    own_out, far_out, near_out = outs
    units, places = [], []
    for m in range(MB):
        v_all, a_all = contexts(data, m)
        for h, cols in heads_of(width):
            v_ctx, a_ctx = v_all[:, cols], a_all[:, cols]
            first, second = m * GROUP, HALF + m * GROUP
            v_cot = jnp.concatenate(
                [cots[first : first + VH, cols], cots[second : second + VH, cols]], axis=0
            )
            a_cot = jnp.concatenate(
                [
                    cots[first + VH : first + GROUP, cols],
                    cots[second + VH : second + GROUP, cols],
                ],
                axis=0,
            )
            v_scale, a_scale = mods[0:1, cols] * SCALE, mods[1:2, cols] * SCALE
            v_own, a_own = v_ctx[VH : 3 * VH], a_ctx[AH : 3 * AH]
            units.append((load(0, m, h), v_cot, v_own, a_ctx, v_scale, mods[2:3, cols]))
            units.append((load(1, m, h), a_cot, a_own, v_ctx, a_scale, mods[3:4, cols]))
            places.append((h, cols, first, second))
    found = attend_back(units)
    by_mods = {}
    for at, (h, cols, first, second) in enumerate(places):
        v_q, a_by, s0, g2 = found[2 * at]
        a_q, v_by, s1, g3 = found[2 * at + 1]
        rows = jnp.concatenate([s0, s1, g2, g3], axis=0)
        by_mods[h] = by_mods[h] + rows if h in by_mods else rows
        v_total = units[2 * at][1] + v_q + v_by[VH : 3 * VH]
        a_total = units[2 * at + 1][1] + a_q + a_by[AH : 3 * AH]
        own_out[first : first + VH, cols] = v_total[:VH]
        own_out[first + VH : first + GROUP, cols] = a_total[:AH]
        own_out[second : second + VH, cols] = v_total[VH:]
        own_out[second + VH : second + GROUP, cols] = a_total[AH:]
        far_out[first : first + VH, cols] = v_by[:VH].astype(BF16)
        far_out[first + VH : first + GROUP, cols] = a_by[:AH].astype(BF16)
        near_out[first : first + VH, cols] = v_by[3 * VH :].astype(BF16)
        near_out[first + VH : first + GROUP, cols] = a_by[3 * AH :].astype(BF16)
    return jnp.concatenate([by_mods[h] for h, _ in heads_of(width)], axis=1)


def top_layer(far_own, near_own, far_in, near_in, extra, cots, own_out, far_out, near_out, mods):
    found = {}

    def store(*key_value):
        found[key_value[:3]] = key_value[3]

    data = (far_own, near_own, far_in, near_in)
    forward_layer(data, extra, store)
    mods[...] = jnp.zeros_like(mods)
    mods[mods.shape[0] - 1] = backward_layer(
        data, extra, cots[...].astype(F32), lambda *key: found[key], (own_out, far_out, near_out)
    )


def weights_ahead(far_own, near_own, far_in, near_in, extra, v_weights, a_weights):
    def store(kind, m, h, value):
        (v_weights, a_weights)[kind][0, m, h] = value

    forward_layer((far_own, near_own, far_in, near_in), extra, store)


def joined(own, far_in, near_in):
    first = own[:HALF].astype(F32) + far_in[...].astype(F32)
    second = own[HALF:].astype(F32) + near_in[...].astype(F32)
    return jnp.concatenate([first, second], axis=0).astype(BF16)


def lower_layer(layer, *refs):
    data, extra, (own, far_part, near_part, v_weights, a_weights, mods_in) = (
        refs[:4],
        refs[4],
        refs[5:11],
    )
    total_out, mods, *outs = refs[11:]
    total = joined(own, far_part, near_part)
    total_out[...] = total
    mods[...] = mods_in[...]
    mods[layer] = backward_layer(
        data,
        extra,
        total.astype(F32),
        lambda kind, m, h: (v_weights, a_weights)[kind][0, m, h],
        outs,
    )


def ahead(mods, *refs):
    totals, (home, spread) = refs[:-2], refs[-2:]
    count = home.shape[0]
    for at, total in enumerate(totals):
        home[count - 1 - at] = total[...]
    copies = spread.shape[0] // count
    for at in range(spread.shape[0]):
        spread[at] = mods[at // copies]


def last_layer(*refs):
    data, extra, (own, far_part, near_part, v_weights, a_weights) = refs[:4], refs[4], refs[5:10]
    home, spread, *outs = refs[12:]
    total = joined(own, far_part, near_part)
    home[0] = total
    found = backward_layer(
        data,
        extra,
        total.astype(F32),
        lambda kind, m, h: (v_weights, a_weights)[kind][0, m, h],
        outs,
    )
    for at in range(spread.shape[0]):
        spread[at] = found


def group_sum(own, moved):
    total = own[...] + moved[0][...]
    return total + (moved[1][...] + moved[2][...]) if len(moved) == 3 else total


def gather_totals(own, far_part, near_part, _, spread, out, mods):
    out[0] = joined(own, far_part, near_part)
    count = mods.shape[2] // own.shape[1]
    copies = spread.shape[0] // count
    chunks = []
    for c in range(count):
        chunks.append(sum((spread[c * copies + i] for i in range(1, copies)), spread[c * copies]))
    mods[0] = jnp.concatenate(chunks, axis=1)


def add_group(own, *refs):
    refs[-1][...] = group_sum(own, refs[:-1])


def finish(received, mods, *refs):
    moved, (video, audio, mods_out) = refs[:-3], refs[-3:]
    mods_out[...] = group_sum(mods, moved)
    count, _, width = received.shape
    seq = lax.axis_index("seq")
    for chunk in range(count):
        columns = pl.ds(chunk * width, width)
        for half in range(2):
            v_rows, a_rows = rows_of(half, seq)
            for m in range(MB):
                base = half * HALF + m * GROUP
                video[0, m, v_rows, columns] = received[chunk, base : base + VH]
                audio[0, m, a_rows, columns] = received[chunk, base + VH : base + GROUP]


def swap(value, first):
    pairs = [(i, i + 1) for i in range(first, lax.axis_size("seq") - 1, 2)]
    return lax.ppermute(value, "seq", pairs + [(b, a) for a, b in pairs])


def swap_near(value):
    return swap(value, 0)


def swap_far(value):
    return swap(value, 1)


def to_section(value, k):
    count = lax.axis_size("section")
    if k == 0:
        return value
    return lax.ppermute(value, "section", [(s, (s + k) % count) for s in range(count)])


def split_bits(count):
    return ((0, 5), ((1, 2), (3, 4))) if count == 64 else ((0,), ((1,),))


def home_and_sum(spread):
    sections, count = lax.axis_size("section"), lax.axis_size("seq")
    bits = split_bits(count)[0]
    mask = sum(1 << bit for bit in bits)
    members = [i for i in range(count) if i & ~mask == 0]
    groups = [
        [s * count + base + i for s in range(sections) for i in members]
        for base in range(count)
        if base & mask == 0
    ]
    return lax.all_to_all(
        spread, ("section", "seq"), 0, 0, axis_index_groups=groups, tiled=True
    )


def group_moves(value, bits):
    count = lax.axis_size("seq")
    masks = [1 << bits[0]]
    if len(bits) == 2:
        masks += [1 << bits[1], 1 << bits[0] | 1 << bits[1]]
    return [lax.ppermute(value, "seq", [(i, i ^ mask) for i in range(count)]) for mask in masks]


def local(video_saved, audio_saved, video_cot, audio_cot, modulation, v_window, a_window):
    sections, count = lax.axis_size("section"), lax.axis_size("seq")
    width = video_saved.shape[3] // sections
    heads = width // HDIM
    flops = 200_000_000

    def whole(*dims):
        return pl.BlockSpec(dims, lambda *_: (0,) * len(dims))

    def like(arrays):
        return [whole(*a.shape) for a in arrays]

    def run(body, arrays, outs, specs=None, **kw):
        return call(
            body,
            tuple(outs),
            grid=(1,),
            in_specs=specs or like(arrays),
            out_specs=tuple(like(outs)),
            **kw,
        )(*arrays)

    hbm = pl.BlockSpec(memory_space=pltpu.HBM)

    def run_prepare(order, arrays, outs, limit):
        return call(
            functools.partial(prepare, order),
            outs,
            grid=(1,),
            in_specs=[hbm] * len(arrays),
            out_specs=tuple(like(outs)),
            limit=limit,
            scratch_shapes=[
                (pltpu.VMEM if a.size > 2 else pltpu.SMEM)(a.shape, a.dtype) for a in arrays
            ]
            + [pltpu.SemaphoreType.DMA((len(arrays),))],
            name="prepare" if order[0] else "prepare_own",
        )(*arrays)

    inputs = (video_saved, audio_saved, modulation, v_window, a_window)
    piece = shape(ROWS + MODS, width)
    order = section_order(sections)
    sent = run_prepare(order[:-1], inputs, (piece,) * (sections - 1), LARGE)
    pieces = [to_section(value, k) for value, k in zip(sent, order)]
    own_piece, cots = run_prepare(
        order[-1:], inputs + (video_cot, audio_cot), (piece, shape(ROWS, width)), OWN_LIMIT
    )
    pieces.append(own_piece)
    far_own, near_own, extra = run(
        assemble,
        tuple(pieces),
        [shape(sections, HALF, width), shape(sections, HALF, width), shape(sections, MODS, width)],
        name="assemble",
    )
    far_in = swap_far(far_own)
    near_in = swap_near(near_own)
    data = (far_own, near_own, far_in, near_in, extra)

    def layer_specs(index):
        return [pl.BlockSpec((1,) + a.shape[1:], lambda *i: (index(*i), 0, 0)) for a in data]

    chain = [
        shape(ROWS, width, dtype=F32),
        shape(HALF, width),
        shape(HALF, width),
        shape(sections, 4, width, dtype=F32),
    ]
    top = sections - 1
    own, far_out, near_out, mods = run(
        top_layer,
        data + (cots,),
        chain,
        layer_specs(lambda *_: top) + like([cots]),
        flops=flops,
        name="top_layer",
    )
    blocks = [(1, MB, heads, 2 * VH, 4 * AH), (1, MB, heads, 2 * AH, 4 * VH)]
    weights = call(
        weights_ahead,
        tuple(shape(top, *block[1:], dtype=F32) for block in blocks),
        flops=3 * flops,
        grid=(top,),
        in_specs=layer_specs(lambda i: i),
        out_specs=tuple(pl.BlockSpec(block, lambda i: (i, 0, 0, 0, 0)) for block in blocks),
        name="weights_ahead",
    )(*data)

    home_bits, steps = split_bits(count)
    spread_shape = shape(sections << len(home_bits), 4, width, dtype=F32)
    anywhere = pl.BlockSpec(memory_space=pl.ANY)
    home_shape = shape(sections, ROWS, width)

    def slot(at):
        return pl.BlockSpec((1, ROWS, width), lambda *_: (at, 0, 0))

    totals = []
    part = (own, swap_far(far_out), swap_near(near_out))
    for layer in reversed(range(top)):
        weight_specs = [pl.BlockSpec(b, lambda *_, at=layer: (at, 0, 0, 0, 0)) for b in blocks]
        specs = layer_specs(lambda *_, at=layer: at) + like(part) + weight_specs
        if layer:
            total, mods, own, far_out, near_out = run(
                functools.partial(lower_layer, layer),
                data + part + tuple(weights) + (mods,),
                [shape(ROWS, width), chain[3]] + chain[:3],
                specs + like([mods]),
                flops=flops,
                name="lower_layer",
            )
            totals.append(total)
        else:
            home, spread = run(
                ahead, (mods, *totals), [home_shape, spread_shape], name="ahead"
            )
            home, spread, own, far_out, near_out = call(
                last_layer,
                (home_shape, spread_shape, *chain[:3]),
                flops=flops,
                grid=(1,),
                in_specs=specs + [anywhere] * 2,
                out_specs=(slot(1), whole(1 << len(home_bits), 4, width), *like(chain[:3])),
                input_output_aliases={10: 0, 11: 1},
                name="last_layer",
            )(*data, *part, *weights, home, spread)
        part = (own, swap_far(far_out), swap_near(near_out))

    mods_shape = shape(1, 4, sections * width, dtype=F32)
    out, mods = call(
        gather_totals,
        (home_shape, mods_shape),
        grid=(1,),
        in_specs=like(part) + [anywhere] + like([spread_shape]),
        out_specs=(slot(0), *like([mods_shape])),
        input_output_aliases={3: 0},
        name="gather_totals",
    )(*part, home, home_and_sum(spread))
    received = lax.all_to_all(out, "section", 0, 0, tiled=True)
    for bits in steps[:-1]:
        (mods,) = run(add_group, (mods, *group_moves(mods, bits)), [mods_shape], name="add_group")
    return tuple(
        run(
            finish,
            (received, mods, *group_moves(mods, steps[-1])),
            [shape(*video_saved.shape), shape(*audio_saved.shape), mods_shape],
            name="finish",
        )
    )


def solution(mesh):
    return jax.shard_map(
        local,
        mesh=mesh,
        in_specs=(
            P("section", None, "seq", None),
            P("section", None, "seq", None),
            P(None, "seq", None),
            P(None, "seq", None),
            P("section", None, None),
            P("seq", None),
            P("seq", None),
        ),
        out_specs=(
            P("section", None, "seq", None),
            P("section", None, "seq", None),
            P("section", None, None),
        ),
        check_vma=False,
    )
```
